256 devices in a mesh: bx: 8 (over z_hi, y), by: 32 (over x, z_lo, core).
Axes of the slice: x: 4, y: 4, z: 8 (z_hi: 2, z_lo: 4; z = z_hi * 4 + z_lo), core: 2. Of those that a mesh axis runs over, the one named last changes fastest.
Arguments:
- weights: bfloat16 [2097152, 128], P(('bx', 'by')), may hold values from -6 to 6
- waves: float32 [2, 2097152], P(None, ('bx', 'by')), may hold values from -4 to 4
- interp: bfloat16 [6, 2, 2, 64, 64], replicated, as said below
Outputs:
- transformed: bfloat16 [2097152, 128], P(('bx', 'by'))
The draws below stay inside these ranges and needn't reach their ends.
Inputs may be any that keep to these rules, and one draw needn't show every extreme that they name: Each matrix interp[l, j, k] has 0.55 on its diagonal plus independent entries of deviation about 0.06.
All inputs are finite; a program needn't handle non-finite values.
Results may differ from the reference program's by a relative error of at most 0.025.
Values may be sent and summed in bfloat16 or wider, within the bound.
A program may use at most 64 MiB of HBM per device.

```python
import math
import jax
import jax.numpy as jnp
from jax import lax

PAIRS_DEV = 8192
NODES = 64
LEVELS = 6
BOXES = 2097152
N_BX = 8
N_BY = 32


def draw_interp(key, part):
    key = jax.random.fold_in(key, 7)
    shape = (LEVELS, 2, 2, NODES, NODES)
    noise = jax.random.normal(key, shape, jnp.float32)
    eye = jnp.eye(NODES, dtype=jnp.float32)
    return (0.55 * eye + 0.06 * noise).astype(jnp.bfloat16)


def block_levels(stream_key, dims, cuts, least, high):
    gain, own = 1.0, jax.random.fold_in(stream_key, 6)
    for axis_at, shards_of in cuts:
        heights = jnp.exp(jax.random.uniform(jax.random.fold_in(own, axis_at), (shards_of,), jnp.float32, least / len(cuts), high / len(cuts)))
        gain = gain * jnp.repeat(heights, dims[axis_at] // shards_of).reshape([-1 if axis == axis_at else 1 for axis in range(len(dims))])
    return gain


def normal_values(stream_key, dims, scale, limit, cuts=(), held_as=jnp.bfloat16):
    drawn = scale * jax.random.normal(stream_key, dims, jnp.float32)
    if cuts:
        drawn = drawn * block_levels(stream_key, dims, cuts, -0.22, 0.18)
    return jnp.clip(drawn, -limit, limit).astype(held_as)


def setup_inputs(seed: int = 0) -> dict:
    key_list = jax.random.split(jax.random.key(seed), 4)
    return {
        "weights": normal_values(key_list[0], (BOXES, 2 * NODES), 1.0, 6.0, ((0, 256),)),
        "waves": jnp.clip(jax.random.uniform(key_list[1], (2, BOXES), jnp.float32, -4.0, 4.0) * block_levels(key_list[1], (2, BOXES), ((1, 256),), -0.4, 0.0), -4.0, 4.0),
        "interp": draw_interp(jax.random.fold_in(key_list[3], 71), 0),
    }


def node_tables():
    index = jnp.arange(64, dtype=jnp.int32)
    first = (index // 8).astype(jnp.float32)
    second = (index % 8).astype(jnp.float32)
    return jnp.cos(math.pi * (first + 0.5) / 8.0), jnp.cos(math.pi * (second + 0.5) / 8.0)


def level_step(state, kx, ky, interp, level, u_nodes, v_nodes):
    if level % 2 == 0:
        dim, count = 0, N_BX
        bit = (level // 2) % (count.bit_length() - 1)
        form = "nmbkq,nqr->nmbkr"
    else:
        dim, count = 1, N_BY
        nbits = count.bit_length() - 1
        bit = nbits - 1 - ((level // 2) % nbits)
        form = "mnbkq,nqr->mnbkr"
    index = jnp.arange(count, dtype=jnp.int32)
    own = (index >> bit) & 1
    partner = jnp.take(state, index ^ (1 << bit), axis=dim)
    mats = interp[level].astype(jnp.float32)
    m_own = mats[own, own]
    m_cross = mats[own, 1 - own]
    shaped = state.reshape(state.shape[:3] + (2, 64)).astype(jnp.float32)
    other = partner.reshape(state.shape[:3] + (2, 64)).astype(jnp.float32)
    local = jnp.einsum(form, shaped, m_own)
    cross = jnp.einsum(form, other, m_cross).astype(jnp.bfloat16)
    cross = lax.optimization_barrier(cross).astype(jnp.float32)
    total = local + cross
    child = own.astype(jnp.float32)
    if dim == 0:
        shift_x = child[:, None, None]
        shift_y = jnp.zeros((1, 1, 1), jnp.float32)
    else:
        shift_x = jnp.zeros((1, 1, 1), jnp.float32)
        shift_y = child[None, :, None]
    scale = 1.0 + 0.25 * level
    theta = scale * ((kx + shift_x)[..., None] * u_nodes + (ky + shift_y)[..., None] * v_nodes)
    cosine = jnp.cos(theta)
    sine = jnp.sin(theta)
    real_part = total[..., 0, :]
    imag_part = total[..., 1, :]
    new_real = real_part * cosine - imag_part * sine
    new_imag = real_part * sine + imag_part * cosine
    return jnp.concatenate([new_real, new_imag], axis=-1).astype(jnp.bfloat16)


def reference(weights, waves, interp):
    block = math.gcd(PAIRS_DEV, 256)
    nblocks = PAIRS_DEV // block
    u_nodes, v_nodes = node_tables()
    state = weights.reshape(N_BX, N_BY, nblocks, block, 128)
    state = jnp.moveaxis(state, 2, 0)
    kx = jnp.moveaxis(waves[0].reshape(N_BX, N_BY, nblocks, block), 2, 0)
    ky = jnp.moveaxis(waves[1].reshape(N_BX, N_BY, nblocks, block), 2, 0)

    def one_block(items):
        block_state, block_kx, block_ky = items
        for level in range(LEVELS):
            block_state = level_step(block_state, block_kx, block_ky, interp, level, u_nodes, v_nodes)
        return block_state

    result = lax.map(one_block, (state, kx, ky))
    result = jnp.moveaxis(result, 0, 2)
    return result.reshape(BOXES, 128)
```

```python
import functools
import math

import jax
import jax.numpy as jnp
import numpy as np
from jax import lax
from jax.experimental import pallas as pl
from jax.experimental.pallas import tpu as pltpu
from jax.sharding import PartitionSpec as P

MESH = pl.DeviceIdType.MESH
LEVELS = 6
CHUNKS = 4
ROWS = 128 // CHUNKS
HALF = ROWS // 2
BITS = (2, 5, 3, 4, 1, 0)


def split3(values):
    values = np.asarray(values, np.float32)
    first = values.astype(jnp.bfloat16).astype(np.float32)
    second = (values - first).astype(jnp.bfloat16).astype(np.float32)
    third = (values - first - second).astype(jnp.bfloat16).astype(np.float32)
    return first, second, third


def tables():
    index = np.arange(64)
    u = np.cos(math.pi * (index // 8 + 0.5) / 8.0)
    v = np.cos(math.pi * (index % 8 + 0.5) / 8.0)
    node = np.zeros((8, 128, 256), np.float32)
    for s in range(8):
        for which, values in enumerate((u, v)):
            hi, mid, lo = split3(values / 8.0)
            for row, part in enumerate((hi, mid, lo, hi, mid, hi)):
                node[s, s * 16 + which * 8 + row, 0:64] = part
                node[s, s * 16 + which * 8 + row, 192:256] = part
    shift = np.zeros((LEVELS, 2, 2, 8, 128), np.float32)
    for level in range(LEVELS):
        angle = (1.0 + 0.25 * level) * (u if level % 2 == 0 else v)
        angle = np.concatenate([angle, angle])
        shift[level, 0, 0] = 1.0
        shift[level, 1, 0] = np.cos(angle)
        shift[level, 1, 1] = np.sin(angle)
    swap = np.zeros((256, 256), np.float32)
    for block, to in enumerate((0, 2, 1, 3)):
        for i in range(64):
            swap[block * 64 + i, to * 64 + i] = 1.0
    place = np.zeros((64, 256), np.float32)
    place[np.arange(64), np.arange(64)] = 1.0
    place[np.arange(64), 192 + np.arange(64)] = 1.0
    as_bf16 = lambda a: jnp.asarray(a, jnp.bfloat16)
    return as_bf16(node), jnp.asarray(shift), as_bf16(swap), as_bf16(place)


def turn(a, b):
    return a[0] * b[0] - a[1] * b[1], a[0] * b[1] + a[1] * b[0]


def double(a):
    both = a[0] * a[1]
    return a[0] * a[0] - a[1] * a[1], both + both


def unit(x):
    y = x * x
    cosine = jnp.full_like(y, -1.0 / 3628800.0)
    for term in (1.0 / 40320.0, -1.0 / 720.0, 1.0 / 24.0, -0.5, 1.0):
        cosine = cosine * y + term
    sine = jnp.full_like(y, 1.0 / 362880.0)
    for term in (-1.0 / 5040.0, 1.0 / 120.0, -1.0 / 6.0, 1.0):
        sine = sine * y + term
    return cosine, sine * x


def kernel(
    w_ref, wave_ref, interp_ref, node_ref, shift_ref, swap_ref, place_ref, o_ref,
    col, here, back, wcol, whole, mats, state, phase, node, shift, swap, place, interp,
    z_send, z_recv, xy_send, xy_recv, yx_send, yx_recv, zo_send, zo_recv, wave_send, wave_recv, load,
):
    bx, by = lax.axis_index("bx"), lax.axis_index("by")
    my_y, z_hi = bx % 4, bx // 4
    my_x, z_mid, low = by // 8, (by // 4) % 2, by % 4
    my_z = z_hi * 2 + z_mid
    my_xy = my_x * 4 + my_y

    def device(z, xy):
        return ((z // 2) * 4 + xy % 4, (xy // 4) * 8 + (z % 2) * 4 + low)

    def along_z(k):
        z = my_z ^ k
        return z, device(z, my_xy)

    def along_xy(k):
        xy = my_xy ^ k
        return xy, device(my_z, xy)

    loads = [
        pltpu.make_async_copy(src, dst, load.at[i])
        for i, (src, dst) in enumerate(
            ((node_ref, node), (shift_ref, shift), (swap_ref, swap), (place_ref, place), (interp_ref, interp))
        )
    ]
    for copy in loads:
        copy.start()

    barrier = pltpu.get_barrier_semaphore()

    def greet(k, carry):
        pl.semaphore_signal(barrier, inc=1, device_id=along_xy(k)[1], device_id_type=MESH)
        return carry

    for k in (1, 2, 3):
        pl.semaphore_signal(barrier, inc=1, device_id=along_z(k)[1], device_id_type=MESH)
    lax.fori_loop(1, 16, greet, 0)
    pl.semaphore_wait(barrier, 18)

    def send(src, dst, send_sem, recv_sem, to):
        pltpu.make_async_remote_copy(
            src_ref=src, dst_ref=dst, send_sem=send_sem, recv_sem=recv_sem, device_id=to, device_id_type=MESH
        ).start()

    def wait(ref, sem):
        pltpu.make_async_copy(ref, ref, sem).wait()

    def waves_of(ref, z):
        return ref.at[:, pl.ds(pl.multiple_of(z * 2048, 2048), 2048)]

    def waves_at(xy):
        return wcol.at[:, :, pl.ds(pl.multiple_of(xy * 128, 128), 128)]

    def z_in(c):
        for k in (1, 2, 3):
            z, to = along_z(k)
            send(w_ref.at[z, :, c], col.at[c, my_z], z_send.at[c], z_recv.at[c], to)
        pltpu.make_async_copy(w_ref.at[my_z, :, c], col.at[c, my_z], z_recv.at[c]).start()

    def xy_in(c):
        def one(k, carry):
            xy, to = along_xy(k)
            send(col.at[c, :, xy], here.at[c, my_xy], xy_send.at[c], xy_recv.at[c], to)
            return carry

        lax.fori_loop(1, 16, one, 0)
        pltpu.make_async_copy(col.at[c, :, my_xy], here.at[c, my_xy], xy_recv.at[c]).start()

    def xy_out(c):
        def one(k, carry):
            xy, to = along_xy(k)
            send(here.at[c, xy], back.at[c, :, my_xy], yx_send.at[c], yx_recv.at[c], to)
            return carry

        lax.fori_loop(1, 16, one, 0)
        pltpu.make_async_copy(here.at[c, my_xy], back.at[c, :, my_xy], yx_recv.at[c]).start()

    def z_out(c):
        for k in (1, 2, 3):
            z, to = along_z(k)
            send(back.at[c, z], o_ref.at[my_z, :, c], zo_send.at[c], zo_recv.at[c], to)
        pltpu.make_async_copy(back.at[c, my_z], o_ref.at[my_z, :, c], zo_recv.at[c]).start()

    for k in (1, 2, 3):
        z, to = along_z(k)
        send(waves_of(wave_ref, z), wcol.at[my_z], wave_send.at[0], wave_recv.at[0], to)
    pltpu.make_async_copy(waves_of(wave_ref, my_z), wcol.at[my_z], wave_recv.at[0]).start()
    for c in range(CHUNKS):
        z_in(c)

    for copy in loads:
        copy.wait()
    for level in range(LEVELS):
        for j in range(2):
            for k in range(2):
                pair = jnp.dot(
                    interp[level * 4 + j * 2 + k], place[...], preferred_element_type=jnp.float32
                ).astype(jnp.bfloat16)
                mats[level, pl.ds(k * 128, 64), pl.ds(j * 128, 128)] = pair[:, :128]
                mats[level, pl.ds(k * 128 + 64, 64), pl.ds(j * 128, 128)] = pair[:, 128:]

    wait(wcol, wave_recv.at[0])

    def wave_in(k, carry):
        xy, to = along_xy(k)
        send(waves_at(xy), whole.at[my_xy], wave_send.at[1], wave_recv.at[1], to)
        return carry

    lax.fori_loop(1, 16, wave_in, 0)
    pltpu.make_async_copy(waves_at(my_xy), whole.at[my_xy], wave_recv.at[1]).start()
    wait(whole, wave_recv.at[1])

    row = lax.broadcasted_iota(jnp.int32, (8, 128), 0)

    def phases(block, carry):
        parts = []
        for s in range(8):
            pair = whole[block * 2 + s // 4, s % 4]
            for which in range(2):
                value = jnp.broadcast_to(pair[which : which + 1], (8, 128))
                hi = value.astype(jnp.bfloat16).astype(jnp.float32)
                mid = (value - hi).astype(jnp.bfloat16).astype(jnp.float32)
                lo = value - hi - mid
                part = jnp.where(row < 3, hi, jnp.where(row < 5, mid, jnp.where(row < 6, lo, 0.0)))
                parts.append(part)
        left = jnp.concatenate(parts, axis=0).T.astype(jnp.bfloat16)
        for s in range(8):
            both = jnp.dot(left, node[s], preferred_element_type=jnp.float32)
            both = both.reshape(CHUNKS, 2, HALF, 256)
            eighth = unit(both[:, 0, :, :128] + both[:, 1, :, 128:])
            quarter = double(eighth)
            now = double(double(quarter))
            for level in range(LEVELS):
                bit = BITS[level]
                child = (s >> bit) & 1 if bit < 3 else (block >> (bit - 3)) & 1
                if level:
                    now = turn(now, quarter)
                step = (
                    jnp.tile(shift[level, child, 0], (HALF // 8, 1)),
                    jnp.tile(shift[level, child, 1], (HALF // 8, 1)),
                )
                out = turn(now, step)
                for part in range(2):
                    phase[level, part, :, block * 8 + s] = out[part]
        return carry

    lax.fori_loop(0, 8, phases, 0)

    def compute(c):
        rows = here[c].reshape(64, 2, HALF, 128)
        both = jnp.concatenate(
            [rows[:, 0].reshape(64 * HALF, 128), rows[:, 1].reshape(64 * HALF, 128)], axis=1
        )
        both = jnp.dot(both, swap[...], preferred_element_type=jnp.float32).astype(jnp.bfloat16)
        state[0] = both[:, :128].reshape(64, HALF, 128)
        state[1] = both[:, 128:].reshape(64, HALF, 128)
        for level in range(LEVELS):
            bit = BITS[level]
            shape = (64 >> (bit + 1), 2, 1 << bit, HALF, 128)
            old = state[...].reshape((2,) + shape)
            left = jnp.concatenate(
                [old[:, :, 0].reshape(64 * HALF, 128), old[:, :, 1].reshape(64 * HALF, 128)], axis=1
            )
            total = jnp.dot(left, mats[level], preferred_element_type=jnp.float32)
            cosine = phase[level, 0, c].reshape(shape)
            sine = phase[level, 1, c].reshape(shape)
            new_real, new_imag = [], []
            for child in range(2):
                part = total[:, child * 128 : child * 128 + 128]
                part = part.reshape((2, shape[0]) + shape[2:])
                real, imag = turn((part[0], part[1]), (cosine[:, child], sine[:, child]))
                new_real.append(real.astype(jnp.bfloat16))
                new_imag.append(imag.astype(jnp.bfloat16))
            state[0] = jnp.stack(new_real, axis=1).reshape(64, HALF, 128)
            state[1] = jnp.stack(new_imag, axis=1).reshape(64, HALF, 128)
        both = jnp.concatenate(
            [state[0].reshape(64 * HALF, 128), state[1].reshape(64 * HALF, 128)], axis=1
        )
        both = jnp.dot(both, swap[...], preferred_element_type=jnp.float32).astype(jnp.bfloat16)
        rows = jnp.stack([both[:, :128].reshape(64, HALF, 128), both[:, 128:].reshape(64, HALF, 128)], axis=1)
        here[c] = rows.reshape(16, 4, ROWS, 128)

    def step(s, carry):
        @pl.when(s < CHUNKS)
        def _():
            wait(col.at[s], z_recv.at[s])
            xy_in(s)

        @pl.when((s >= 1) & (s < CHUNKS + 1))
        def _():
            c = s - 1
            wait(here.at[c], xy_recv.at[c])
            compute(c)
            xy_out(c)

        @pl.when(s >= 2)
        def _():
            c = s - 2
            wait(back.at[c], yx_recv.at[c])
            z_out(c)

        return carry

    lax.fori_loop(0, CHUNKS + 2, step, 0)

    def finish(c, carry):
        wait(o_ref.at[:, :, c], zo_recv.at[c])
        wait(col.at[c, pl.ds(0, 3)], z_send.at[c])
        wait(back.at[c, pl.ds(0, 3)], zo_send.at[c])
        wait(here.at[c, pl.ds(0, 15)], xy_send.at[c])
        wait(here.at[c, pl.ds(0, 15)], yx_send.at[c])
        return carry

    lax.fori_loop(0, CHUNKS, finish, 0)
    wait(wcol.at[pl.ds(0, 3)], wave_send.at[0])
    wait(whole.at[pl.ds(0, 15)], wave_send.at[1])


def body(weights, waves, interp):
    node, shift, swap, place = tables()
    any_space = pl.BlockSpec(memory_space=pl.ANY)
    sems = pltpu.SemaphoreType.DMA((CHUNKS,))
    out = pl.pallas_call(
        kernel,
        out_shape=jax.ShapeDtypeStruct((4, 16, CHUNKS, ROWS, 128), jnp.bfloat16),
        in_specs=[any_space] * 7,
        out_specs=any_space,
        scratch_shapes=[
            pltpu.VMEM((CHUNKS, 4, 16, ROWS, 128), jnp.bfloat16),
            pltpu.VMEM((CHUNKS, 16, 4, ROWS, 128), jnp.bfloat16),
            pltpu.VMEM((CHUNKS, 4, 16, ROWS, 128), jnp.bfloat16),
            pltpu.VMEM((4, 2, 2048), jnp.float32),
            pltpu.VMEM((16, 4, 2, 128), jnp.float32),
            pltpu.VMEM((LEVELS, 256, 256), jnp.bfloat16),
            pltpu.VMEM((2, 64, HALF, 128), jnp.bfloat16),
            pltpu.VMEM((LEVELS, 2, CHUNKS, 64, HALF, 128), jnp.float32),
            pltpu.VMEM(node.shape, node.dtype),
            pltpu.VMEM(shift.shape, shift.dtype),
            pltpu.VMEM(swap.shape, swap.dtype),
            pltpu.VMEM(place.shape, place.dtype),
            pltpu.VMEM((24, 64, 64), jnp.bfloat16),
            sems, sems, sems, sems, sems, sems, sems, sems,
            pltpu.SemaphoreType.DMA((2,)),
            pltpu.SemaphoreType.DMA((2,)),
            pltpu.SemaphoreType.DMA((5,)),
        ],
        compiler_params=pltpu.CompilerParams(
            collective_id=0, has_side_effects=True, vmem_limit_bytes=56 << 20
        ),
    )(weights.reshape(4, 16, CHUNKS, ROWS, 128), waves, interp.reshape(24, 64, 64), node, shift, swap, place)
    return out.reshape(8192, 128)


def solution(mesh):
    return jax.shard_map(
        body,
        mesh=mesh,
        in_specs=(P(("bx", "by"), None), P(None, ("bx", "by")), P()),
        out_specs=P(("bx", "by"), None),
        check_vma=False,
    )
```

```python
import functools
import math

import jax
import jax.numpy as jnp
import numpy as np
from jax import lax
from jax.experimental import pallas as pl
from jax.experimental.pallas import tpu as pltpu
from jax.sharding import PartitionSpec as P

MESH = pl.DeviceIdType.MESH
LEVELS = 6
CHUNKS = 4
ROWS = 128 // CHUNKS
HALF = ROWS // 2
BITS = (2, 5, 3, 4, 1, 0)


def split3(values):
    values = np.asarray(values, np.float32)
    first = values.astype(jnp.bfloat16).astype(np.float32)
    second = (values - first).astype(jnp.bfloat16).astype(np.float32)
    third = (values - first - second).astype(jnp.bfloat16).astype(np.float32)
    return first, second, third


def tables():
    index = np.arange(64)
    u = np.cos(math.pi * (index // 8 + 0.5) / 8.0)
    v = np.cos(math.pi * (index % 8 + 0.5) / 8.0)
    node = np.zeros((8, 128, 256), np.float32)
    for s in range(8):
        for which, values in enumerate((u, v)):
            hi, mid, lo = split3(values / 8.0)
            for row, part in enumerate((hi, mid, lo, hi, mid, hi)):
                node[s, s * 16 + which * 8 + row, 0:64] = part
                node[s, s * 16 + which * 8 + row, 192:256] = part
    shift = np.zeros((LEVELS, 2, 2, 8, 128), np.float32)
    for level in range(LEVELS):
        angle = (1.0 + 0.25 * level) * (u if level % 2 == 0 else v)
        angle = np.concatenate([angle, angle])
        shift[level, 0, 0] = 1.0
        shift[level, 1, 0] = np.cos(angle)
        shift[level, 1, 1] = np.sin(angle)
    swap = np.zeros((256, 256), np.float32)
    for block, to in enumerate((0, 2, 1, 3)):
        for i in range(64):
            swap[block * 64 + i, to * 64 + i] = 1.0
    place = np.zeros((64, 256), np.float32)
    place[np.arange(64), np.arange(64)] = 1.0
    place[np.arange(64), 192 + np.arange(64)] = 1.0
    as_bf16 = lambda a: jnp.asarray(a, jnp.bfloat16)
    return as_bf16(node), jnp.asarray(shift), as_bf16(swap), as_bf16(place)


def turn(a, b):
    return a[0] * b[0] - a[1] * b[1], a[0] * b[1] + a[1] * b[0]


def double(a):
    both = a[0] * a[1]
    return a[0] * a[0] - a[1] * a[1], both + both


def unit(x):
    y = x * x
    cosine = jnp.full_like(y, -1.0 / 3628800.0)
    for term in (1.0 / 40320.0, -1.0 / 720.0, 1.0 / 24.0, -0.5, 1.0):
        cosine = cosine * y + term
    sine = jnp.full_like(y, 1.0 / 362880.0)
    for term in (-1.0 / 5040.0, 1.0 / 120.0, -1.0 / 6.0, 1.0):
        sine = sine * y + term
    return cosine, sine * x


def kernel(
    w_ref, wave_ref, interp_ref, node_ref, shift_ref, swap_ref, place_ref, o_ref,
    col, here, back, wcol, whole, mats, state, phase, node, shift, swap, place, interp,
    z_send, z_recv, xy_send, xy_recv, yx_send, yx_recv, zo_send, zo_recv, wave_send, wave_recv, load,
):
    bx, by = lax.axis_index("bx"), lax.axis_index("by")
    my_y, z_hi = bx % 4, bx // 4
    my_x, z_mid, low = by // 8, (by // 4) % 2, by % 4
    my_z = z_hi * 2 + z_mid
    my_xy = my_x * 4 + my_y

    def device(z, xy):
        return ((z // 2) * 4 + xy % 4, (xy // 4) * 8 + (z % 2) * 4 + low)

    def along_z(k):
        z = my_z ^ k
        return z, device(z, my_xy)

    def along_xy(k):
        xy = my_xy ^ k
        return xy, device(my_z, xy)

    loads = [
        pltpu.make_async_copy(src, dst, load.at[i])
        for i, (src, dst) in enumerate(
            ((node_ref, node), (shift_ref, shift), (swap_ref, swap), (place_ref, place), (interp_ref, interp))
        )
    ]
    for copy in loads:
        copy.start()

    barrier = pltpu.get_barrier_semaphore()

    def greet(k, carry):
        pl.semaphore_signal(barrier, inc=1, device_id=along_xy(k)[1], device_id_type=MESH)
        return carry

    for k in (3, 2, 1):
        pl.semaphore_signal(barrier, inc=1, device_id=along_z(k)[1], device_id_type=MESH)
    lax.fori_loop(1, 16, greet, 0)
    pl.semaphore_wait(barrier, 18)

    def send(src, dst, send_sem, recv_sem, to):
        pltpu.make_async_remote_copy(
            src_ref=src, dst_ref=dst, send_sem=send_sem, recv_sem=recv_sem, device_id=to, device_id_type=MESH
        ).start()

    def wait(ref, sem):
        pltpu.make_async_copy(ref, ref, sem).wait()

    def waves_of(ref, z):
        return ref.at[:, pl.ds(pl.multiple_of(z * 2048, 2048), 2048)]

    def waves_at(xy):
        return wcol.at[:, :, pl.ds(pl.multiple_of(xy * 128, 128), 128)]

    def z_in(c):
        for k in (3, 2, 1):
            z, to = along_z(k)
            send(w_ref.at[z, :, c], col.at[c, my_z], z_send.at[c], z_recv.at[c], to)
        pltpu.make_async_copy(w_ref.at[my_z, :, c], col.at[c, my_z], z_recv.at[c]).start()

    def xy_in(c):
        def one(k, carry):
            xy, to = along_xy(k)
            send(col.at[c, :, xy], here.at[c, my_xy], xy_send.at[c], xy_recv.at[c], to)
            return carry

        lax.fori_loop(1, 16, one, 0)
        pltpu.make_async_copy(col.at[c, :, my_xy], here.at[c, my_xy], xy_recv.at[c]).start()

    def xy_out(c):
        def one(k, carry):
            xy, to = along_xy(k)
            send(here.at[c, xy], back.at[c, :, my_xy], yx_send.at[c], yx_recv.at[c], to)
            return carry

        lax.fori_loop(1, 16, one, 0)
        pltpu.make_async_copy(here.at[c, my_xy], back.at[c, :, my_xy], yx_recv.at[c]).start()

    def z_out(c):
        for k in (3, 2, 1):
            z, to = along_z(k)
            send(back.at[c, z], o_ref.at[my_z, :, c], zo_send.at[c], zo_recv.at[c], to)
        pltpu.make_async_copy(back.at[c, my_z], o_ref.at[my_z, :, c], zo_recv.at[c]).start()

    for k in (3, 2, 1):
        z, to = along_z(k)
        send(waves_of(wave_ref, z), wcol.at[my_z], wave_send.at[0], wave_recv.at[0], to)
    pltpu.make_async_copy(waves_of(wave_ref, my_z), wcol.at[my_z], wave_recv.at[0]).start()
    for c in range(CHUNKS):
        z_in(c)

    for copy in loads:
        copy.wait()
    for level in range(LEVELS):
        for j in range(2):
            for k in range(2):
                pair = jnp.dot(
                    interp[level * 4 + j * 2 + k], place[...], preferred_element_type=jnp.float32
                ).astype(jnp.bfloat16)
                mats[level, pl.ds(k * 128, 64), pl.ds(j * 128, 128)] = pair[:, :128]
                mats[level, pl.ds(k * 128 + 64, 64), pl.ds(j * 128, 128)] = pair[:, 128:]

    wait(wcol, wave_recv.at[0])

    def wave_in(k, carry):
        xy, to = along_xy(k)
        send(waves_at(xy), whole.at[my_xy], wave_send.at[1], wave_recv.at[1], to)
        return carry

    lax.fori_loop(1, 16, wave_in, 0)
    pltpu.make_async_copy(waves_at(my_xy), whole.at[my_xy], wave_recv.at[1]).start()
    wait(whole, wave_recv.at[1])

    row = lax.broadcasted_iota(jnp.int32, (8, 128), 0)

    def phases(block, carry):
        parts = []
        for s in range(8):
            pair = whole[block * 2 + s // 4, s % 4]
            for which in range(2):
                value = jnp.broadcast_to(pair[which : which + 1], (8, 128))
                hi = value.astype(jnp.bfloat16).astype(jnp.float32)
                mid = (value - hi).astype(jnp.bfloat16).astype(jnp.float32)
                lo = value - hi - mid
                part = jnp.where(row < 3, hi, jnp.where(row < 5, mid, jnp.where(row < 6, lo, 0.0)))
                parts.append(part)
        left = jnp.concatenate(parts, axis=0).T.astype(jnp.bfloat16)
        for s in range(8):
            both = jnp.dot(left, node[s], preferred_element_type=jnp.float32)
            both = both.reshape(CHUNKS, 2, HALF, 256)
            eighth = unit(both[:, 0, :, :128] + both[:, 1, :, 128:])
            quarter = double(eighth)
            now = double(double(quarter))
            for level in range(LEVELS):
                bit = BITS[level]
                child = (s >> bit) & 1 if bit < 3 else (block >> (bit - 3)) & 1
                if level:
                    now = turn(now, quarter)
                step = (
                    jnp.tile(shift[level, child, 0], (HALF // 8, 1)),
                    jnp.tile(shift[level, child, 1], (HALF // 8, 1)),
                )
                out = turn(now, step)
                for part in range(2):
                    phase[level, part, :, block * 8 + s] = out[part]
        return carry

    lax.fori_loop(0, 8, phases, 0)

    def compute(c):
        rows = here[c].reshape(64, 2, HALF, 128)
        both = jnp.concatenate(
            [rows[:, 0].reshape(64 * HALF, 128), rows[:, 1].reshape(64 * HALF, 128)], axis=1
        )
        both = jnp.dot(both, swap[...], preferred_element_type=jnp.float32).astype(jnp.bfloat16)
        state[0] = both[:, :128].reshape(64, HALF, 128)
        state[1] = both[:, 128:].reshape(64, HALF, 128)
        for level in range(LEVELS):
            bit = BITS[level]
            shape = (64 >> (bit + 1), 2, 1 << bit, HALF, 128)
            old = state[...].reshape((2,) + shape)
            left = jnp.concatenate(
                [old[:, :, 0].reshape(64 * HALF, 128), old[:, :, 1].reshape(64 * HALF, 128)], axis=1
            )
            total = jnp.dot(left, mats[level], preferred_element_type=jnp.float32)
            cosine = phase[level, 0, c].reshape(shape)
            sine = phase[level, 1, c].reshape(shape)
            new_real, new_imag = [], []
            for child in range(2):
                part = total[:, child * 128 : child * 128 + 128]
                part = part.reshape((2, shape[0]) + shape[2:])
                real, imag = turn((part[0], part[1]), (cosine[:, child], sine[:, child]))
                new_real.append(real.astype(jnp.bfloat16))
                new_imag.append(imag.astype(jnp.bfloat16))
            state[0] = jnp.stack(new_real, axis=1).reshape(64, HALF, 128)
            state[1] = jnp.stack(new_imag, axis=1).reshape(64, HALF, 128)
        both = jnp.concatenate(
            [state[0].reshape(64 * HALF, 128), state[1].reshape(64 * HALF, 128)], axis=1
        )
        both = jnp.dot(both, swap[...], preferred_element_type=jnp.float32).astype(jnp.bfloat16)
        rows = jnp.stack([both[:, :128].reshape(64, HALF, 128), both[:, 128:].reshape(64, HALF, 128)], axis=1)
        here[c] = rows.reshape(16, 4, ROWS, 128)

    def step(s, carry):
        @pl.when(s < CHUNKS)
        def _():
            wait(col.at[s], z_recv.at[s])
            xy_in(s)

        @pl.when((s >= 1) & (s < CHUNKS + 1))
        def _():
            c = s - 1
            wait(here.at[c], xy_recv.at[c])
            compute(c)
            xy_out(c)

        @pl.when(s >= 2)
        def _():
            c = s - 2
            wait(back.at[c], yx_recv.at[c])
            z_out(c)

        return carry

    lax.fori_loop(0, CHUNKS + 2, step, 0)

    def finish(c, carry):
        wait(o_ref.at[:, :, c], zo_recv.at[c])
        wait(col.at[c, pl.ds(0, 3)], z_send.at[c])
        wait(back.at[c, pl.ds(0, 3)], zo_send.at[c])
        wait(here.at[c, pl.ds(0, 15)], xy_send.at[c])
        wait(here.at[c, pl.ds(0, 15)], yx_send.at[c])
        return carry

    lax.fori_loop(0, CHUNKS, finish, 0)
    wait(wcol.at[pl.ds(0, 3)], wave_send.at[0])
    wait(whole.at[pl.ds(0, 15)], wave_send.at[1])


def settle(src_ref, dst_ref, held, arrive, leave):
    parts = [pl.ds(i * 1024, 1024) for i in range(8)]
    for i, part in enumerate(parts):
        pltpu.make_async_copy(src_ref.at[part], held.at[part], arrive.at[i]).start()
    for i, part in enumerate(parts):
        pltpu.make_async_copy(src_ref.at[part], held.at[part], arrive.at[i]).wait()
        pltpu.make_async_copy(held.at[part], dst_ref.at[part], leave.at[i]).start()
    for i, part in enumerate(parts):
        pltpu.make_async_copy(held.at[part], dst_ref.at[part], leave.at[i]).wait()


def body(weights, waves, interp):
    node, shift, swap, place = tables()
    any_space = pl.BlockSpec(memory_space=pl.ANY)
    sems = pltpu.SemaphoreType.DMA((CHUNKS,))
    out = pl.pallas_call(
        kernel,
        out_shape=jax.ShapeDtypeStruct((4, 16, CHUNKS, ROWS, 128), jnp.bfloat16),
        in_specs=[any_space] * 7,
        out_specs=any_space,
        scratch_shapes=[
            pltpu.VMEM((CHUNKS, 4, 16, ROWS, 128), jnp.bfloat16),
            pltpu.VMEM((CHUNKS, 16, 4, ROWS, 128), jnp.bfloat16),
            pltpu.VMEM((CHUNKS, 4, 16, ROWS, 128), jnp.bfloat16),
            pltpu.VMEM((4, 2, 2048), jnp.float32),
            pltpu.VMEM((16, 4, 2, 128), jnp.float32),
            pltpu.VMEM((LEVELS, 256, 256), jnp.bfloat16),
            pltpu.VMEM((2, 64, HALF, 128), jnp.bfloat16),
            pltpu.VMEM((LEVELS, 2, CHUNKS, 64, HALF, 128), jnp.float32),
            pltpu.VMEM(node.shape, node.dtype),
            pltpu.VMEM(shift.shape, shift.dtype),
            pltpu.VMEM(swap.shape, swap.dtype),
            pltpu.VMEM(place.shape, place.dtype),
            pltpu.VMEM((24, 64, 64), jnp.bfloat16),
            sems, sems, sems, sems, sems, sems, sems, sems,
            pltpu.SemaphoreType.DMA((2,)),
            pltpu.SemaphoreType.DMA((2,)),
            pltpu.SemaphoreType.DMA((5,)),
        ],
        compiler_params=pltpu.CompilerParams(
            collective_id=0, has_side_effects=True, vmem_limit_bytes=56 << 20
        ),
    )(weights.reshape(4, 16, CHUNKS, ROWS, 128), waves, interp.reshape(24, 64, 64), node, shift, swap, place)
    return pl.pallas_call(
        settle,
        out_shape=jax.ShapeDtypeStruct((8192, 128), jnp.bfloat16),
        in_specs=[any_space],
        out_specs=any_space,
        scratch_shapes=[
            pltpu.VMEM((8192, 128), jnp.bfloat16),
            pltpu.SemaphoreType.DMA((8,)),
            pltpu.SemaphoreType.DMA((8,)),
        ],
        compiler_params=pltpu.CompilerParams(vmem_limit_bytes=60 << 20),
    )(out.reshape(8192, 128))


def solution(mesh):
    return jax.shard_map(
        body,
        mesh=mesh,
        in_specs=(P(("bx", "by"), None), P(None, ("bx", "by")), P()),
        out_specs=P(("bx", "by"), None),
        check_vma=False,
    )
```

```python
import functools
import math

import jax
import jax.numpy as jnp
import numpy as np
from jax import lax
from jax.experimental import pallas as pl
from jax.experimental.pallas import tpu as pltpu
from jax.sharding import PartitionSpec as P

MESH = pl.DeviceIdType.MESH
LEVELS = 6
CHUNKS = 8
AHEAD = 8
ROWS = 128 // CHUNKS
PAIRS = 32 * ROWS
BITS = (1, 4, 2, 3, 0)


def split3(values):
    values = np.asarray(values, np.float32)
    first = values.astype(jnp.bfloat16).astype(np.float32)
    second = (values - first).astype(jnp.bfloat16).astype(np.float32)
    third = (values - first - second).astype(jnp.bfloat16).astype(np.float32)
    return first, second, third


def tables():
    index = np.arange(64)
    u = np.cos(math.pi * (index // 8 + 0.5) / 8.0)
    v = np.cos(math.pi * (index % 8 + 0.5) / 8.0)
    node = np.zeros((2, 128, 256), np.float32)
    for s in range(8):
        for which, values in enumerate((u, v)):
            hi, mid, lo = split3(values / 8.0)
            for row, part in enumerate((hi, mid, lo, hi, mid, hi)):
                node[s // 4, s * 16 + which * 8 + row, s % 4 * 64 : s % 4 * 64 + 64] = part
    shift = np.zeros((LEVELS, 2, 2, 8, 128), np.float32)
    for level in range(LEVELS):
        angle = (1.0 + 0.25 * level) * (u if level % 2 == 0 else v)
        angles = np.stack([0.0 * angle, angle])
        for child in range(2):
            pair = angles if level == LEVELS - 1 else angles[[child, child]]
            shift[level, child, 0] = np.cos(pair.reshape(128))
            shift[level, child, 1] = np.sin(pair.reshape(128))
    swap = np.zeros((256, 256), np.float32)
    for block, to in enumerate((0, 2, 1, 3)):
        for i in range(64):
            swap[block * 64 + i, to * 64 + i] = 1.0
    place = np.zeros((64, 256), np.float32)
    place[np.arange(64), np.arange(64)] = 1.0
    place[np.arange(64), 192 + np.arange(64)] = 1.0
    as_bf16 = lambda a: jnp.asarray(a, jnp.bfloat16)
    return as_bf16(node), jnp.asarray(shift), as_bf16(swap), as_bf16(place)


def turn(a, b):
    return a[0] * b[0] - a[1] * b[1], a[0] * b[1] + a[1] * b[0]


def double(a):
    both = a[0] * a[1]
    return a[0] * a[0] - a[1] * a[1], both + both


def unit(x):
    y = x * x
    cosine = jnp.full_like(y, -1.0 / 3628800.0)
    for term in (1.0 / 40320.0, -1.0 / 720.0, 1.0 / 24.0, -0.5, 1.0):
        cosine = cosine * y + term
    sine = jnp.full_like(y, 1.0 / 362880.0)
    for term in (-1.0 / 5040.0, 1.0 / 120.0, -1.0 / 6.0, 1.0):
        sine = sine * y + term
    return cosine, sine * x


def kernel(
    w_ref, wave_ref, interp_ref, node_ref, shift_ref, swap_ref, place_ref, o_ref,
    col, here, back, wcol, whole, mats, state, phase, node, shift, swap, place, interp,
    z_send, z_recv, xy_send, xy_recv, yx_send, yx_recv, zo_send, zo_recv, wave_send, wave_recv, load,
):
    bx, by = lax.axis_index("bx"), lax.axis_index("by")
    my_y, z_hi = bx % 4, bx // 4
    my_x, z_mid, low = by // 8, (by // 4) % 2, by % 4
    my_z = z_hi * 2 + z_mid
    my_xy = my_x * 4 + my_y

    def device(z, xy):
        return ((z // 2) * 4 + xy % 4, (xy // 4) * 8 + (z % 2) * 4 + low)

    def along_z(k):
        z = my_z ^ k
        return z, device(z, my_xy)

    def along_xy(k):
        xy = my_xy ^ k
        return xy, device(my_z, xy)

    loads = [
        pltpu.make_async_copy(src, dst, load.at[i])
        for i, (src, dst) in enumerate(
            ((node_ref, node), (shift_ref, shift), (swap_ref, swap), (place_ref, place), (interp_ref, interp))
        )
    ]
    for copy in loads:
        copy.start()

    barrier = pltpu.get_barrier_semaphore()

    def greet(k, carry):
        pl.semaphore_signal(barrier, inc=1, device_id=along_xy(k)[1], device_id_type=MESH)
        return carry

    for k in (3, 2, 1):
        pl.semaphore_signal(barrier, inc=1, device_id=along_z(k)[1], device_id_type=MESH)
    lax.fori_loop(1, 16, greet, 0)
    pl.semaphore_wait(barrier, 18)

    def send(src, dst, send_sem, recv_sem, to):
        pltpu.make_async_remote_copy(
            src_ref=src, dst_ref=dst, send_sem=send_sem, recv_sem=recv_sem, device_id=to, device_id_type=MESH
        ).start()

    def wait(ref, sem):
        pltpu.make_async_copy(ref, ref, sem).wait()

    def waves_of(ref, z):
        return ref.at[:, pl.ds(pl.multiple_of(z * 2048, 2048), 2048)]

    def waves_at(xy):
        return wcol.at[:, :, pl.ds(pl.multiple_of(xy * 128, 128), 128)]

    def z_in(c):
        for k in (3, 2, 1):
            z, to = along_z(k)
            send(w_ref.at[z, :, c], col.at[c, my_z], z_send.at[c], z_recv.at[c], to)
        pltpu.make_async_copy(w_ref.at[my_z, :, c], col.at[c, my_z], z_recv.at[c]).start()

    def xy_in(c):
        def one(k, carry):
            xy, to = along_xy(k)
            send(col.at[c, :, xy], here.at[c, my_xy], xy_send.at[c], xy_recv.at[c], to)
            return carry

        lax.fori_loop(1, 16, one, 0)
        pltpu.make_async_copy(col.at[c, :, my_xy], here.at[c, my_xy], xy_recv.at[c]).start()

    def xy_out(c):
        def one(k, carry):
            xy, to = along_xy(k)
            send(here.at[c, xy], back.at[c, :, my_xy], yx_send.at[c], yx_recv.at[c], to)
            return carry

        lax.fori_loop(1, 16, one, 0)
        pltpu.make_async_copy(here.at[c, my_xy], back.at[c, :, my_xy], yx_recv.at[c]).start()

    def z_out(c):
        for k in (2, 1, 3):
            z, to = along_z(k)
            send(back.at[c, z], o_ref.at[my_z, :, c], zo_send.at[c], zo_recv.at[c], to)
        pltpu.make_async_copy(back.at[c, my_z], o_ref.at[my_z, :, c], zo_recv.at[c]).start()

    for k in (3, 2, 1):
        z, to = along_z(k)
        send(waves_of(wave_ref, z), wcol.at[my_z], wave_send.at[0], wave_recv.at[0], to)
    pltpu.make_async_copy(waves_of(wave_ref, my_z), wcol.at[my_z], wave_recv.at[0]).start()
    for c in range(AHEAD):
        z_in(c)

    for copy in loads:
        copy.wait()
    last = [[None, None], [None, None]]
    for level in range(LEVELS):
        for j in range(2):
            for k in range(2):
                pair = jnp.dot(
                    interp[level * 4 + j * 2 + k], place[...], preferred_element_type=jnp.float32
                ).astype(jnp.bfloat16)
                if level < LEVELS - 1:
                    mats[level, pl.ds(k * 128, 64), pl.ds(j * 128, 128)] = pair[:, :128]
                    mats[level, pl.ds(k * 128 + 64, 64), pl.ds(j * 128, 128)] = pair[:, 128:]
                else:
                    last[k][j] = pair

    for k in range(2):
        block = (last[k][0][:, :128].astype(jnp.float32) + last[k][1][:, 128:].astype(jnp.float32)).astype(jnp.bfloat16)
        empty = jnp.zeros((64, 128), jnp.bfloat16)
        mats[LEVELS - 1, pl.ds(k * 64, 64), pl.ds(0, 128)] = block
        mats[LEVELS - 1, pl.ds(k * 64, 64), pl.ds(128, 128)] = empty
        mats[LEVELS - 1, pl.ds(128 + k * 64, 64), pl.ds(0, 128)] = empty
        mats[LEVELS - 1, pl.ds(128 + k * 64, 64), pl.ds(128, 128)] = block

    wait(wcol, wave_recv.at[0])

    def wave_in(k, carry):
        xy, to = along_xy(k)
        send(waves_at(xy), whole.at[my_xy], wave_send.at[1], wave_recv.at[1], to)
        return carry

    lax.fori_loop(1, 16, wave_in, 0)
    pltpu.make_async_copy(waves_at(my_xy), whole.at[my_xy], wave_recv.at[1]).start()
    wait(whole, wave_recv.at[1])

    row = lax.broadcasted_iota(jnp.int32, (8, 128), 0)

    def phases(block, carry):
        parts = []
        for s in range(8):
            pair = whole[block * 2 + s // 4, s % 4]
            for which in range(2):
                value = jnp.broadcast_to(pair[which : which + 1], (8, 128))
                hi = value.astype(jnp.bfloat16).astype(jnp.float32)
                mid = (value - hi).astype(jnp.bfloat16).astype(jnp.float32)
                lo = value - hi - mid
                part = jnp.where(row < 3, hi, jnp.where(row < 5, mid, jnp.where(row < 6, lo, 0.0)))
                parts.append(part)
        left = jnp.concatenate(parts, axis=0).T.astype(jnp.bfloat16)
        for half in range(2):
            four = jnp.dot(left, node[half], preferred_element_type=jnp.float32)
            for side in range(2):
                t = half * 2 + side
                eighth = unit(four[:, side * 128 : side * 128 + 128].reshape(CHUNKS, ROWS, 128))
                quarter = double(eighth)
                now = double(double(quarter))
                for level in range(LEVELS):
                    bit = BITS[level] if level < LEVELS - 1 else 0
                    child = (t >> bit) & 1 if bit < 2 else (block >> (bit - 2)) & 1
                    if level:
                        now = turn(now, quarter)
                    step = (
                        jnp.tile(shift[level, child, 0], (ROWS // 8, 1)),
                        jnp.tile(shift[level, child, 1], (ROWS // 8, 1)),
                    )
                    out = turn(now, step)
                    for part in range(2):
                        phase[level, part, :, block * 4 + t] = out[part]
        return carry

    lax.fori_loop(0, 8, phases, 0)

    def compute(c):
        rows = here[c].reshape(32, 2, ROWS, 128)
        both = jnp.concatenate(
            [rows[:, 0].reshape(PAIRS, 128), rows[:, 1].reshape(PAIRS, 128)], axis=1
        )
        both = jnp.dot(both, swap[...], preferred_element_type=jnp.float32).astype(jnp.bfloat16)
        state[0] = both[:, :128].reshape(32, ROWS, 128)
        state[1] = both[:, 128:].reshape(32, ROWS, 128)
        for level in range(LEVELS - 1):
            bit = BITS[level]
            shape = (32 >> (bit + 1), 2, 1 << bit, ROWS, 128)
            old = state[...].reshape((2,) + shape)
            left = jnp.concatenate(
                [old[:, :, 0].reshape(PAIRS, 128), old[:, :, 1].reshape(PAIRS, 128)], axis=1
            )
            total = jnp.dot(left, mats[level], preferred_element_type=jnp.float32)
            cosine = phase[level, 0, c].reshape(shape)
            sine = phase[level, 1, c].reshape(shape)
            new_real, new_imag = [], []
            for child in range(2):
                part = total[:, child * 128 : child * 128 + 128]
                part = part.reshape((2, shape[0]) + shape[2:])
                real, imag = turn((part[0], part[1]), (cosine[:, child], sine[:, child]))
                new_real.append(real.astype(jnp.bfloat16))
                new_imag.append(imag.astype(jnp.bfloat16))
            state[0] = jnp.stack(new_real, axis=1).reshape(32, ROWS, 128)
            state[1] = jnp.stack(new_imag, axis=1).reshape(32, ROWS, 128)
        both = jnp.concatenate([state[0].reshape(PAIRS, 128), state[1].reshape(PAIRS, 128)], axis=1)
        total = jnp.dot(both, mats[LEVELS - 1], preferred_element_type=jnp.float32)
        real, imag = turn(
            (total[:, :128], total[:, 128:]),
            (phase[LEVELS - 1, 0, c].reshape(PAIRS, 128), phase[LEVELS - 1, 1, c].reshape(PAIRS, 128)),
        )
        both = jnp.concatenate([real.astype(jnp.bfloat16), imag.astype(jnp.bfloat16)], axis=1)
        both = jnp.dot(both, swap[...], preferred_element_type=jnp.float32).astype(jnp.bfloat16)
        rows = jnp.stack([both[:, :128].reshape(32, ROWS, 128), both[:, 128:].reshape(32, ROWS, 128)], axis=1)
        here[c] = rows.reshape(16, 4, ROWS, 128)

    def step(s, carry):
        @pl.when(s < CHUNKS)
        def _():
            wait(col.at[s], z_recv.at[s])
            xy_in(s)

        @pl.when(s < CHUNKS - AHEAD)
        def _():
            z_in(s + AHEAD)

        @pl.when((s >= 1) & (s < CHUNKS + 1))
        def _():
            c = s - 1
            wait(here.at[c], xy_recv.at[c])
            compute(c)
            xy_out(c)

        @pl.when(s >= 4)
        def _():
            c = s - 4
            wait(back.at[c], yx_recv.at[c])
            z_out(c)

        return carry

    lax.fori_loop(0, CHUNKS + 4, step, 0)

    def finish(c, carry):
        wait(o_ref.at[:, :, c], zo_recv.at[c])
        wait(col.at[c, pl.ds(0, 3)], z_send.at[c])
        wait(back.at[c, pl.ds(0, 3)], zo_send.at[c])
        wait(here.at[c, pl.ds(0, 15)], xy_send.at[c])
        wait(here.at[c, pl.ds(0, 15)], yx_send.at[c])
        return carry

    lax.fori_loop(0, CHUNKS, finish, 0)
    wait(wcol.at[pl.ds(0, 3)], wave_send.at[0])
    wait(whole.at[pl.ds(0, 15)], wave_send.at[1])


def settle(src_ref, dst_ref, held, arrive, leave):
    parts = [pl.ds(i * 1024, 1024) for i in range(8)]
    for i, part in enumerate(parts):
        pltpu.make_async_copy(src_ref.at[part], held.at[part], arrive.at[i]).start()
    for i, part in enumerate(parts):
        pltpu.make_async_copy(src_ref.at[part], held.at[part], arrive.at[i]).wait()
        pltpu.make_async_copy(held.at[part], dst_ref.at[part], leave.at[i]).start()
    for i, part in enumerate(parts):
        pltpu.make_async_copy(held.at[part], dst_ref.at[part], leave.at[i]).wait()


def body(weights, waves, interp):
    node, shift, swap, place = tables()
    any_space = pl.BlockSpec(memory_space=pl.ANY)
    sems = pltpu.SemaphoreType.DMA((CHUNKS,))
    out = pl.pallas_call(
        kernel,
        out_shape=jax.ShapeDtypeStruct((4, 16, CHUNKS, ROWS, 128), jnp.bfloat16),
        in_specs=[any_space] * 7,
        out_specs=any_space,
        scratch_shapes=[
            pltpu.VMEM((CHUNKS, 4, 16, ROWS, 128), jnp.bfloat16),
            pltpu.VMEM((CHUNKS, 16, 4, ROWS, 128), jnp.bfloat16),
            pltpu.VMEM((CHUNKS, 4, 16, ROWS, 128), jnp.bfloat16),
            pltpu.VMEM((4, 2, 2048), jnp.float32),
            pltpu.VMEM((16, 4, 2, 128), jnp.float32),
            pltpu.VMEM((LEVELS, 256, 256), jnp.bfloat16),
            pltpu.VMEM((2, 32, ROWS, 128), jnp.bfloat16),
            pltpu.VMEM((LEVELS, 2, CHUNKS, 32, ROWS, 128), jnp.float32),
            pltpu.VMEM(node.shape, node.dtype),
            pltpu.VMEM(shift.shape, shift.dtype),
            pltpu.VMEM(swap.shape, swap.dtype),
            pltpu.VMEM(place.shape, place.dtype),
            pltpu.VMEM((24, 64, 64), jnp.bfloat16),
            sems, sems, sems, sems, sems, sems, sems, sems,
            pltpu.SemaphoreType.DMA((2,)),
            pltpu.SemaphoreType.DMA((2,)),
            pltpu.SemaphoreType.DMA((5,)),
        ],
        compiler_params=pltpu.CompilerParams(
            collective_id=0, has_side_effects=True, vmem_limit_bytes=56 << 20
        ),
    )(weights.reshape(4, 16, CHUNKS, ROWS, 128), waves, interp.reshape(24, 64, 64), node, shift, swap, place)
    return pl.pallas_call(
        settle,
        out_shape=jax.ShapeDtypeStruct((8192, 128), jnp.bfloat16),
        in_specs=[any_space],
        out_specs=any_space,
        scratch_shapes=[
            pltpu.VMEM((8192, 128), jnp.bfloat16),
            pltpu.SemaphoreType.DMA((8,)),
            pltpu.SemaphoreType.DMA((8,)),
        ],
        compiler_params=pltpu.CompilerParams(vmem_limit_bytes=60 << 20),
    )(out.reshape(8192, 128))


def solution(mesh):
    return jax.shard_map(
        body,
        mesh=mesh,
        in_specs=(P(("bx", "by"), None), P(None, ("bx", "by")), P()),
        out_specs=P(("bx", "by"), None),
        check_vma=False,
    )
```

```python
import functools
import math

import jax
import jax.numpy as jnp
import numpy as np
from jax import lax
from jax.experimental import pallas as pl
from jax.experimental.pallas import tpu as pltpu
from jax.sharding import PartitionSpec as P

MESH = pl.DeviceIdType.MESH
LEVELS = 6
CHUNKS = 8
AHEAD = 8
ROWS = 128 // CHUNKS
PAIRS = 32 * ROWS
BITS = (1, 4, 2, 3, 0)


def split3(values):
    values = np.asarray(values, np.float32)
    first = values.astype(jnp.bfloat16).astype(np.float32)
    second = (values - first).astype(jnp.bfloat16).astype(np.float32)
    third = (values - first - second).astype(jnp.bfloat16).astype(np.float32)
    return first, second, third


def tables():
    index = np.arange(64)
    u = np.cos(math.pi * (index // 8 + 0.5) / 8.0)
    v = np.cos(math.pi * (index % 8 + 0.5) / 8.0)
    node = np.zeros((2, 128, 256), np.float32)
    for s in range(8):
        for which, values in enumerate((u, v)):
            hi, mid, lo = split3(values / 8.0)
            for row, part in enumerate((hi, mid, lo, hi, mid, hi)):
                node[s // 4, s * 16 + which * 8 + row, s % 4 * 64 : s % 4 * 64 + 64] = part
    shift = np.zeros((LEVELS, 2, 2, 8, 128), np.float32)
    for level in range(LEVELS):
        angle = (1.0 + 0.25 * level) * (u if level % 2 == 0 else v)
        angles = np.stack([0.0 * angle, angle])
        for child in range(2):
            pair = angles if level == LEVELS - 1 else angles[[child, child]]
            shift[level, child, 0] = np.cos(pair.reshape(128))
            shift[level, child, 1] = np.sin(pair.reshape(128))
    swap = np.zeros((256, 256), np.float32)
    for block, to in enumerate((0, 2, 1, 3)):
        for i in range(64):
            swap[block * 64 + i, to * 64 + i] = 1.0
    place = np.zeros((64, 256), np.float32)
    place[np.arange(64), np.arange(64)] = 1.0
    place[np.arange(64), 192 + np.arange(64)] = 1.0
    as_bf16 = lambda a: jnp.asarray(a, jnp.bfloat16)
    return as_bf16(node), jnp.asarray(shift), as_bf16(swap), as_bf16(place)


def turn(a, b):
    return a[0] * b[0] - a[1] * b[1], a[0] * b[1] + a[1] * b[0]


def double(a):
    both = a[0] * a[1]
    return a[0] * a[0] - a[1] * a[1], both + both


def unit(x):
    y = x * x
    cosine = jnp.full_like(y, -1.0 / 3628800.0)
    for term in (1.0 / 40320.0, -1.0 / 720.0, 1.0 / 24.0, -0.5, 1.0):
        cosine = cosine * y + term
    sine = jnp.full_like(y, 1.0 / 362880.0)
    for term in (-1.0 / 5040.0, 1.0 / 120.0, -1.0 / 6.0, 1.0):
        sine = sine * y + term
    return cosine, sine * x


def kernel(
    w_ref, wave_ref, interp_ref, node_ref, shift_ref, swap_ref, place_ref, o_ref,
    col, here, back, wcol, whole, mats, state, phase, node, shift, swap, place, interp,
    z_send, z_recv, xy_send, xy_recv, yx_send, yx_recv, zo_send, zo_recv, wave_send, wave_recv, load,
):
    bx, by = lax.axis_index("bx"), lax.axis_index("by")
    my_y, z_hi = bx % 4, bx // 4
    my_x, z_mid, low = by // 8, (by // 4) % 2, by % 4
    my_z = z_hi * 2 + z_mid
    my_xy = my_x * 4 + my_y

    def device(z, xy):
        return ((z // 2) * 4 + xy % 4, (xy // 4) * 8 + (z % 2) * 4 + low)

    def along_z(k):
        z = my_z ^ k
        return z, device(z, my_xy)

    def along_xy(k):
        xy = my_xy ^ k
        return xy, device(my_z, xy)

    loads = [
        pltpu.make_async_copy(src, dst, load.at[i])
        for i, (src, dst) in enumerate(
            ((node_ref, node), (shift_ref, shift), (swap_ref, swap), (place_ref, place), (interp_ref, interp))
        )
    ]
    barrier = pltpu.get_barrier_semaphore()

    def greet(k, carry):
        pl.semaphore_signal(barrier, inc=1, device_id=along_xy(k)[1], device_id_type=MESH)
        return carry

    for k in (3, 2, 1):
        pl.semaphore_signal(barrier, inc=1, device_id=along_z(k)[1], device_id_type=MESH)
    lax.fori_loop(1, 16, greet, 0)
    pl.semaphore_wait(barrier, 18)

    def send(src, dst, send_sem, recv_sem, to):
        pltpu.make_async_remote_copy(
            src_ref=src, dst_ref=dst, send_sem=send_sem, recv_sem=recv_sem, device_id=to, device_id_type=MESH
        ).start()

    def wait(ref, sem):
        pltpu.make_async_copy(ref, ref, sem).wait()

    def waves_of(ref, z):
        return ref.at[:, pl.ds(pl.multiple_of(z * 2048, 2048), 2048)]

    def waves_at(xy):
        return wcol.at[:, :, pl.ds(pl.multiple_of(xy * 128, 128), 128)]

    def z_in(c):
        for k in (3, 2, 1):
            z, to = along_z(k)
            send(w_ref.at[z, :, c], col.at[c, my_z], z_send.at[c], z_recv.at[c], to)
        pltpu.make_async_copy(w_ref.at[my_z, :, c], col.at[c, my_z], z_recv.at[c]).start()

    def xy_in(c):
        def one(k, carry):
            xy, to = along_xy(k)
            send(col.at[c, :, xy], here.at[c, my_xy], xy_send.at[c], xy_recv.at[c], to)
            return carry

        lax.fori_loop(1, 16, one, 0)
        pltpu.make_async_copy(col.at[c, :, my_xy], here.at[c, my_xy], xy_recv.at[c]).start()

    def xy_out(c):
        def one(k, carry):
            xy, to = along_xy(k)
            send(here.at[c, xy], back.at[c, :, my_xy], yx_send.at[c], yx_recv.at[c], to)
            return carry

        lax.fori_loop(1, 16, one, 0)
        pltpu.make_async_copy(here.at[c, my_xy], back.at[c, :, my_xy], yx_recv.at[c]).start()

    def z_out(c):
        for k in (2, 1, 3):
            z, to = along_z(k)
            send(back.at[c, z], o_ref.at[my_z, :, c], zo_send.at[c], zo_recv.at[c], to)
        pltpu.make_async_copy(back.at[c, my_z], o_ref.at[my_z, :, c], zo_recv.at[c]).start()

    for k in (3, 2, 1):
        z, to = along_z(k)
        send(waves_of(wave_ref, z), wcol.at[my_z], wave_send.at[0], wave_recv.at[0], to)
    pltpu.make_async_copy(waves_of(wave_ref, my_z), wcol.at[my_z], wave_recv.at[0]).start()
    for c in range(AHEAD):
        z_in(c)
    for copy in loads:
        copy.start()

    for copy in loads:
        copy.wait()
    last = [[None, None], [None, None]]
    for level in range(LEVELS):
        for j in range(2):
            for k in range(2):
                pair = jnp.dot(
                    interp[level * 4 + j * 2 + k], place[...], preferred_element_type=jnp.float32
                ).astype(jnp.bfloat16)
                if level < LEVELS - 1:
                    mats[level, pl.ds(k * 128, 64), pl.ds(j * 128, 128)] = pair[:, :128]
                    mats[level, pl.ds(k * 128 + 64, 64), pl.ds(j * 128, 128)] = pair[:, 128:]
                else:
                    last[k][j] = pair

    for k in range(2):
        block = (last[k][0][:, :128].astype(jnp.float32) + last[k][1][:, 128:].astype(jnp.float32)).astype(jnp.bfloat16)
        empty = jnp.zeros((64, 128), jnp.bfloat16)
        mats[LEVELS - 1, pl.ds(k * 64, 64), pl.ds(0, 128)] = block
        mats[LEVELS - 1, pl.ds(k * 64, 64), pl.ds(128, 128)] = empty
        mats[LEVELS - 1, pl.ds(128 + k * 64, 64), pl.ds(0, 128)] = empty
        mats[LEVELS - 1, pl.ds(128 + k * 64, 64), pl.ds(128, 128)] = block

    wait(wcol, wave_recv.at[0])

    def wave_in(k, carry):
        xy, to = along_xy(k)
        send(waves_at(xy), whole.at[my_xy], wave_send.at[1], wave_recv.at[1], to)
        return carry

    lax.fori_loop(1, 16, wave_in, 0)
    pltpu.make_async_copy(waves_at(my_xy), whole.at[my_xy], wave_recv.at[1]).start()
    wait(whole, wave_recv.at[1])

    row = lax.broadcasted_iota(jnp.int32, (8, 128), 0)

    def phases(block, carry):
        parts = []
        for s in range(8):
            pair = whole[block * 2 + s // 4, s % 4]
            for which in range(2):
                value = jnp.broadcast_to(pair[which : which + 1], (8, 128))
                hi = value.astype(jnp.bfloat16).astype(jnp.float32)
                mid = (value - hi).astype(jnp.bfloat16).astype(jnp.float32)
                lo = value - hi - mid
                part = jnp.where(row < 3, hi, jnp.where(row < 5, mid, jnp.where(row < 6, lo, 0.0)))
                parts.append(part)
        left = jnp.concatenate(parts, axis=0).T.astype(jnp.bfloat16)
        for half in range(2):
            four = jnp.dot(left, node[half], preferred_element_type=jnp.float32)
            for side in range(2):
                t = half * 2 + side
                eighth = unit(four[:, side * 128 : side * 128 + 128].reshape(CHUNKS, ROWS, 128))
                quarter = double(eighth)
                now = double(double(quarter))
                for level in range(LEVELS):
                    bit = BITS[level] if level < LEVELS - 1 else 0
                    child = (t >> bit) & 1 if bit < 2 else (block >> (bit - 2)) & 1
                    if level:
                        now = turn(now, quarter)
                    step = (
                        jnp.tile(shift[level, child, 0], (ROWS // 8, 1)),
                        jnp.tile(shift[level, child, 1], (ROWS // 8, 1)),
                    )
                    out = turn(now, step)
                    for part in range(2):
                        phase[level, part, :, block * 4 + t] = out[part]
        return carry

    lax.fori_loop(0, 8, phases, 0)

    def compute(c):
        rows = here[c].reshape(32, 2, ROWS, 128)
        both = jnp.concatenate(
            [rows[:, 0].reshape(PAIRS, 128), rows[:, 1].reshape(PAIRS, 128)], axis=1
        )
        both = jnp.dot(both, swap[...], preferred_element_type=jnp.float32).astype(jnp.bfloat16)
        state[0] = both[:, :128].reshape(32, ROWS, 128)
        state[1] = both[:, 128:].reshape(32, ROWS, 128)
        for level in range(LEVELS - 1):
            bit = BITS[level]
            shape = (32 >> (bit + 1), 2, 1 << bit, ROWS, 128)
            old = state[...].reshape((2,) + shape)
            left = jnp.concatenate(
                [old[:, :, 0].reshape(PAIRS, 128), old[:, :, 1].reshape(PAIRS, 128)], axis=1
            )
            total = jnp.dot(left, mats[level], preferred_element_type=jnp.float32)
            cosine = phase[level, 0, c].reshape(shape)
            sine = phase[level, 1, c].reshape(shape)
            new_real, new_imag = [], []
            for child in range(2):
                part = total[:, child * 128 : child * 128 + 128]
                part = part.reshape((2, shape[0]) + shape[2:])
                real, imag = turn((part[0], part[1]), (cosine[:, child], sine[:, child]))
                new_real.append(real.astype(jnp.bfloat16))
                new_imag.append(imag.astype(jnp.bfloat16))
            state[0] = jnp.stack(new_real, axis=1).reshape(32, ROWS, 128)
            state[1] = jnp.stack(new_imag, axis=1).reshape(32, ROWS, 128)
        both = jnp.concatenate([state[0].reshape(PAIRS, 128), state[1].reshape(PAIRS, 128)], axis=1)
        total = jnp.dot(both, mats[LEVELS - 1], preferred_element_type=jnp.float32)
        real, imag = turn(
            (total[:, :128], total[:, 128:]),
            (phase[LEVELS - 1, 0, c].reshape(PAIRS, 128), phase[LEVELS - 1, 1, c].reshape(PAIRS, 128)),
        )
        both = jnp.concatenate([real.astype(jnp.bfloat16), imag.astype(jnp.bfloat16)], axis=1)
        both = jnp.dot(both, swap[...], preferred_element_type=jnp.float32).astype(jnp.bfloat16)
        rows = jnp.stack([both[:, :128].reshape(32, ROWS, 128), both[:, 128:].reshape(32, ROWS, 128)], axis=1)
        here[c] = rows.reshape(16, 4, ROWS, 128)

    def step(s, carry):
        @pl.when(s < CHUNKS)
        def _():
            wait(col.at[s], z_recv.at[s])
            xy_in(s)

        @pl.when(s < CHUNKS - AHEAD)
        def _():
            z_in(s + AHEAD)

        @pl.when((s >= 1) & (s < CHUNKS + 1))
        def _():
            c = s - 1
            wait(here.at[c], xy_recv.at[c])
            compute(c)
            xy_out(c)

        @pl.when(s >= 4)
        def _():
            c = s - 4
            wait(back.at[c], yx_recv.at[c])
            z_out(c)

        return carry

    lax.fori_loop(0, CHUNKS + 4, step, 0)

    def finish(c, carry):
        wait(o_ref.at[:, :, c], zo_recv.at[c])
        wait(col.at[c, pl.ds(0, 3)], z_send.at[c])
        wait(back.at[c, pl.ds(0, 3)], zo_send.at[c])
        wait(here.at[c, pl.ds(0, 15)], xy_send.at[c])
        wait(here.at[c, pl.ds(0, 15)], yx_send.at[c])
        return carry

    lax.fori_loop(0, CHUNKS, finish, 0)
    wait(wcol.at[pl.ds(0, 3)], wave_send.at[0])
    wait(whole.at[pl.ds(0, 15)], wave_send.at[1])


def settle(src_ref, dst_ref, held, arrive, leave):
    parts = [pl.ds(i * 1024, 1024) for i in range(8)]
    for i, part in enumerate(parts):
        pltpu.make_async_copy(src_ref.at[part], held.at[part], arrive.at[i]).start()
    for i, part in enumerate(parts):
        pltpu.make_async_copy(src_ref.at[part], held.at[part], arrive.at[i]).wait()
        pltpu.make_async_copy(held.at[part], dst_ref.at[part], leave.at[i]).start()
    for i, part in enumerate(parts):
        pltpu.make_async_copy(held.at[part], dst_ref.at[part], leave.at[i]).wait()


def body(weights, waves, interp):
    node, shift, swap, place = tables()
    any_space = pl.BlockSpec(memory_space=pl.ANY)
    sems = pltpu.SemaphoreType.DMA((CHUNKS,))
    out = pl.pallas_call(
        kernel,
        out_shape=jax.ShapeDtypeStruct((4, 16, CHUNKS, ROWS, 128), jnp.bfloat16),
        in_specs=[any_space] * 7,
        out_specs=any_space,
        scratch_shapes=[
            pltpu.VMEM((CHUNKS, 4, 16, ROWS, 128), jnp.bfloat16),
            pltpu.VMEM((CHUNKS, 16, 4, ROWS, 128), jnp.bfloat16),
            pltpu.VMEM((CHUNKS, 4, 16, ROWS, 128), jnp.bfloat16),
            pltpu.VMEM((4, 2, 2048), jnp.float32),
            pltpu.VMEM((16, 4, 2, 128), jnp.float32),
            pltpu.VMEM((LEVELS, 256, 256), jnp.bfloat16),
            pltpu.VMEM((2, 32, ROWS, 128), jnp.bfloat16),
            pltpu.VMEM((LEVELS, 2, CHUNKS, 32, ROWS, 128), jnp.float32),
            pltpu.VMEM(node.shape, node.dtype),
            pltpu.VMEM(shift.shape, shift.dtype),
            pltpu.VMEM(swap.shape, swap.dtype),
            pltpu.VMEM(place.shape, place.dtype),
            pltpu.VMEM((24, 64, 64), jnp.bfloat16),
            sems, sems, sems, sems, sems, sems, sems, sems,
            pltpu.SemaphoreType.DMA((2,)),
            pltpu.SemaphoreType.DMA((2,)),
            pltpu.SemaphoreType.DMA((5,)),
        ],
        compiler_params=pltpu.CompilerParams(
            collective_id=0, has_side_effects=True, vmem_limit_bytes=56 << 20
        ),
    )(weights.reshape(4, 16, CHUNKS, ROWS, 128), waves, interp.reshape(24, 64, 64), node, shift, swap, place)
    return pl.pallas_call(
        settle,
        out_shape=jax.ShapeDtypeStruct((8192, 128), jnp.bfloat16),
        in_specs=[any_space],
        out_specs=any_space,
        scratch_shapes=[
            pltpu.VMEM((8192, 128), jnp.bfloat16),
            pltpu.SemaphoreType.DMA((8,)),
            pltpu.SemaphoreType.DMA((8,)),
        ],
        compiler_params=pltpu.CompilerParams(vmem_limit_bytes=60 << 20),
    )(out.reshape(8192, 128))


def solution(mesh):
    return jax.shard_map(
        body,
        mesh=mesh,
        in_specs=(P(("bx", "by"), None), P(None, ("bx", "by")), P()),
        out_specs=P(("bx", "by"), None),
        check_vma=False,
    )
```

```python
import functools
import math

import jax
import jax.numpy as jnp
import numpy as np
from jax import lax
from jax.experimental import pallas as pl
from jax.experimental.pallas import tpu as pltpu
from jax.sharding import PartitionSpec as P

MESH = pl.DeviceIdType.MESH
LEVELS = 6
CHUNKS = 8
AHEAD = 8
ROWS = 128 // CHUNKS
PAIRS = 32 * ROWS
BITS = (1, 4, 2, 3, 0)


def split3(values):
    values = np.asarray(values, np.float32)
    first = values.astype(jnp.bfloat16).astype(np.float32)
    second = (values - first).astype(jnp.bfloat16).astype(np.float32)
    third = (values - first - second).astype(jnp.bfloat16).astype(np.float32)
    return first, second, third


def tables():
    index = np.arange(64)
    u = np.cos(math.pi * (index // 8 + 0.5) / 8.0)
    v = np.cos(math.pi * (index % 8 + 0.5) / 8.0)
    node = np.zeros((2, 128, 256), np.float32)
    for s in range(8):
        for which, values in enumerate((u, v)):
            hi, mid, lo = split3(values / 8.0)
            for row, part in enumerate((hi, mid, lo, hi, mid, hi)):
                node[s // 4, s * 16 + which * 8 + row, s % 4 * 64 : s % 4 * 64 + 64] = part
    shift = np.zeros((LEVELS, 2, 2, 8, 128), np.float32)
    for level in range(LEVELS):
        angle = (1.0 + 0.25 * level) * (u if level % 2 == 0 else v)
        angles = np.stack([0.0 * angle, angle])
        for child in range(2):
            pair = angles if level == LEVELS - 1 else angles[[child, child]]
            shift[level, child, 0] = np.cos(pair.reshape(128))
            shift[level, child, 1] = np.sin(pair.reshape(128))
    swap = np.zeros((256, 256), np.float32)
    for block, to in enumerate((0, 2, 1, 3)):
        for i in range(64):
            swap[block * 64 + i, to * 64 + i] = 1.0
    place = np.zeros((64, 256), np.float32)
    place[np.arange(64), np.arange(64)] = 1.0
    place[np.arange(64), 192 + np.arange(64)] = 1.0
    as_bf16 = lambda a: jnp.asarray(a, jnp.bfloat16)
    return as_bf16(node), jnp.asarray(shift), as_bf16(swap), as_bf16(place)


def turn(a, b):
    return a[0] * b[0] - a[1] * b[1], a[0] * b[1] + a[1] * b[0]


def double(a):
    both = a[0] * a[1]
    return a[0] * a[0] - a[1] * a[1], both + both


def unit(x):
    y = x * x
    cosine = jnp.full_like(y, -1.0 / 3628800.0)
    for term in (1.0 / 40320.0, -1.0 / 720.0, 1.0 / 24.0, -0.5, 1.0):
        cosine = cosine * y + term
    sine = jnp.full_like(y, 1.0 / 362880.0)
    for term in (-1.0 / 5040.0, 1.0 / 120.0, -1.0 / 6.0, 1.0):
        sine = sine * y + term
    return cosine, sine * x


def kernel(
    w_ref, wave_ref, interp_ref, node_ref, shift_ref, swap_ref, place_ref, o_ref,
    col, here, back, wcol, whole, mats, state, phase, node, shift, swap, place, interp,
    z_send, z_recv, xy_send, xy_recv, yx_send, yx_recv, zo_send, zo_recv, wave_send, wave_recv, load,
):
    bx, by = lax.axis_index("bx"), lax.axis_index("by")
    my_y, z_hi = bx % 4, bx // 4
    my_x, z_mid, low = by // 8, (by // 4) % 2, by % 4
    my_z = z_hi * 2 + z_mid
    my_xy = my_x * 4 + my_y

    def device(z, xy):
        return ((z // 2) * 4 + xy % 4, (xy // 4) * 8 + (z % 2) * 4 + low)

    def along_z(k):
        z = my_z ^ k
        return z, device(z, my_xy)

    def along_xy(k):
        xy = my_xy ^ k
        return xy, device(my_z, xy)

    loads = [
        pltpu.make_async_copy(src, dst, load.at[i])
        for i, (src, dst) in enumerate(
            ((node_ref, node), (shift_ref, shift), (swap_ref, swap), (place_ref, place), (interp_ref, interp))
        )
    ]
    barrier = pltpu.get_barrier_semaphore()

    def greet(k, carry):
        pl.semaphore_signal(barrier, inc=1, device_id=along_xy(k)[1], device_id_type=MESH)
        return carry

    for k in (3, 2, 1):
        pl.semaphore_signal(barrier, inc=1, device_id=along_z(k)[1], device_id_type=MESH)
    lax.fori_loop(1, 16, greet, 0)
    pl.semaphore_wait(barrier, 18)

    def send(src, dst, send_sem, recv_sem, to):
        pltpu.make_async_remote_copy(
            src_ref=src, dst_ref=dst, send_sem=send_sem, recv_sem=recv_sem, device_id=to, device_id_type=MESH
        ).start()

    def wait(ref, sem):
        pltpu.make_async_copy(ref, ref, sem).wait()

    def waves_of(ref, z):
        return ref.at[:, pl.ds(pl.multiple_of(z * 2048, 2048), 2048)]

    def waves_at(xy):
        return wcol.at[:, :, pl.ds(pl.multiple_of(xy * 128, 128), 128)]

    def z_in(c):
        for k in (3, 2, 1):
            z, to = along_z(k)
            send(w_ref.at[z, :, c], col.at[c, my_z], z_send.at[c], z_recv.at[c], to)

    def xy_in(c):
        def one(k, carry):
            xy, to = along_xy(k)
            send(col.at[c, :, xy], here.at[c, my_xy], xy_send.at[c], xy_recv.at[c], to)
            return carry

        lax.fori_loop(1, 16, one, 0)
        pltpu.make_async_copy(col.at[c, :, my_xy], here.at[c, my_xy], xy_recv.at[c]).start()

    def xy_out(c):
        def one(k, carry):
            xy, to = along_xy(k)
            send(here.at[c, xy], back.at[c, :, my_xy], yx_send.at[c], yx_recv.at[c], to)
            return carry

        lax.fori_loop(1, 16, one, 0)
        pltpu.make_async_copy(here.at[c, my_xy], back.at[c, :, my_xy], yx_recv.at[c]).start()

    def z_out(c):
        for k in (2, 1, 3):
            z, to = along_z(k)
            send(back.at[c, z], o_ref.at[my_z, :, c], zo_send.at[c], zo_recv.at[c], to)
        pltpu.make_async_copy(back.at[c, my_z], o_ref.at[my_z, :, c], zo_recv.at[c]).start()

    for k in (3, 2, 1):
        z, to = along_z(k)
        send(waves_of(wave_ref, z), wcol.at[my_z], wave_send.at[0], wave_recv.at[0], to)
    pltpu.make_async_copy(waves_of(wave_ref, my_z), wcol.at[my_z], wave_recv.at[0]).start()
    for c in range(CHUNKS):
        pltpu.make_async_copy(w_ref.at[my_z, :, c], col.at[c, my_z], z_recv.at[c]).start()
    for c in range(AHEAD):
        z_in(c)
    for copy in loads:
        copy.start()

    for copy in loads:
        copy.wait()
    last = [[None, None], [None, None]]
    for level in range(LEVELS):
        for j in range(2):
            for k in range(2):
                pair = jnp.dot(
                    interp[level * 4 + j * 2 + k], place[...], preferred_element_type=jnp.float32
                ).astype(jnp.bfloat16)
                if level < LEVELS - 1:
                    mats[level, pl.ds(k * 128, 64), pl.ds(j * 128, 128)] = pair[:, :128]
                    mats[level, pl.ds(k * 128 + 64, 64), pl.ds(j * 128, 128)] = pair[:, 128:]
                else:
                    last[k][j] = pair

    for k in range(2):
        block = (last[k][0][:, :128].astype(jnp.float32) + last[k][1][:, 128:].astype(jnp.float32)).astype(jnp.bfloat16)
        empty = jnp.zeros((64, 128), jnp.bfloat16)
        mats[LEVELS - 1, pl.ds(k * 64, 64), pl.ds(0, 128)] = block
        mats[LEVELS - 1, pl.ds(k * 64, 64), pl.ds(128, 128)] = empty
        mats[LEVELS - 1, pl.ds(128 + k * 64, 64), pl.ds(0, 128)] = empty
        mats[LEVELS - 1, pl.ds(128 + k * 64, 64), pl.ds(128, 128)] = block

    wait(wcol, wave_recv.at[0])

    def wave_in(k, carry):
        xy, to = along_xy(k)
        send(waves_at(xy), whole.at[my_xy], wave_send.at[1], wave_recv.at[1], to)
        return carry

    lax.fori_loop(1, 16, wave_in, 0)
    pltpu.make_async_copy(waves_at(my_xy), whole.at[my_xy], wave_recv.at[1]).start()
    wait(whole, wave_recv.at[1])

    row = lax.broadcasted_iota(jnp.int32, (8, 128), 0)

    def phases(block, carry):
        parts = []
        for s in range(8):
            pair = whole[block * 2 + s // 4, s % 4]
            for which in range(2):
                value = jnp.broadcast_to(pair[which : which + 1], (8, 128))
                hi = value.astype(jnp.bfloat16).astype(jnp.float32)
                mid = (value - hi).astype(jnp.bfloat16).astype(jnp.float32)
                lo = value - hi - mid
                part = jnp.where(row < 3, hi, jnp.where(row < 5, mid, jnp.where(row < 6, lo, 0.0)))
                parts.append(part)
        left = jnp.concatenate(parts, axis=0).T.astype(jnp.bfloat16)
        for half in range(2):
            four = jnp.dot(left, node[half], preferred_element_type=jnp.float32)
            for side in range(2):
                t = half * 2 + side
                eighth = unit(four[:, side * 128 : side * 128 + 128].reshape(CHUNKS, ROWS, 128))
                quarter = double(eighth)
                now = double(double(quarter))
                for level in range(LEVELS):
                    bit = BITS[level] if level < LEVELS - 1 else 0
                    child = (t >> bit) & 1 if bit < 2 else (block >> (bit - 2)) & 1
                    if level:
                        now = turn(now, quarter)
                    step = (
                        jnp.tile(shift[level, child, 0], (ROWS // 8, 1)),
                        jnp.tile(shift[level, child, 1], (ROWS // 8, 1)),
                    )
                    out = turn(now, step)
                    for part in range(2):
                        phase[level, part, :, block * 4 + t] = out[part]
        return carry

    lax.fori_loop(0, 8, phases, 0)

    def compute(c):
        rows = here[c].reshape(32, 2, ROWS, 128)
        both = jnp.concatenate(
            [rows[:, 0].reshape(PAIRS, 128), rows[:, 1].reshape(PAIRS, 128)], axis=1
        )
        both = jnp.dot(both, swap[...], preferred_element_type=jnp.float32).astype(jnp.bfloat16)
        state[0] = both[:, :128].reshape(32, ROWS, 128)
        state[1] = both[:, 128:].reshape(32, ROWS, 128)
        for level in range(LEVELS - 1):
            bit = BITS[level]
            shape = (32 >> (bit + 1), 2, 1 << bit, ROWS, 128)
            old = state[...].reshape((2,) + shape)
            left = jnp.concatenate(
                [old[:, :, 0].reshape(PAIRS, 128), old[:, :, 1].reshape(PAIRS, 128)], axis=1
            )
            total = jnp.dot(left, mats[level], preferred_element_type=jnp.float32)
            cosine = phase[level, 0, c].reshape(shape)
            sine = phase[level, 1, c].reshape(shape)
            new_real, new_imag = [], []
            for child in range(2):
                part = total[:, child * 128 : child * 128 + 128]
                part = part.reshape((2, shape[0]) + shape[2:])
                real, imag = turn((part[0], part[1]), (cosine[:, child], sine[:, child]))
                new_real.append(real.astype(jnp.bfloat16))
                new_imag.append(imag.astype(jnp.bfloat16))
            state[0] = jnp.stack(new_real, axis=1).reshape(32, ROWS, 128)
            state[1] = jnp.stack(new_imag, axis=1).reshape(32, ROWS, 128)
        both = jnp.concatenate([state[0].reshape(PAIRS, 128), state[1].reshape(PAIRS, 128)], axis=1)
        total = jnp.dot(both, mats[LEVELS - 1], preferred_element_type=jnp.float32)
        real, imag = turn(
            (total[:, :128], total[:, 128:]),
            (phase[LEVELS - 1, 0, c].reshape(PAIRS, 128), phase[LEVELS - 1, 1, c].reshape(PAIRS, 128)),
        )
        both = jnp.concatenate([real.astype(jnp.bfloat16), imag.astype(jnp.bfloat16)], axis=1)
        both = jnp.dot(both, swap[...], preferred_element_type=jnp.float32).astype(jnp.bfloat16)
        rows = jnp.stack([both[:, :128].reshape(32, ROWS, 128), both[:, 128:].reshape(32, ROWS, 128)], axis=1)
        here[c] = rows.reshape(16, 4, ROWS, 128)

    def step(s, carry):
        @pl.when(s < CHUNKS)
        def _():
            wait(col.at[s], z_recv.at[s])
            xy_in(s)

        @pl.when(s < CHUNKS - AHEAD)
        def _():
            z_in(s + AHEAD)

        @pl.when((s >= 1) & (s < CHUNKS + 1))
        def _():
            c = s - 1
            wait(here.at[c], xy_recv.at[c])
            compute(c)
            xy_out(c)

        @pl.when(s >= 4)
        def _():
            c = s - 4
            wait(back.at[c], yx_recv.at[c])
            z_out(c)

        return carry

    lax.fori_loop(0, CHUNKS + 4, step, 0)

    def finish(c, carry):
        wait(o_ref.at[:, :, c], zo_recv.at[c])
        wait(col.at[c, pl.ds(0, 3)], z_send.at[c])
        wait(back.at[c, pl.ds(0, 3)], zo_send.at[c])
        wait(here.at[c, pl.ds(0, 15)], xy_send.at[c])
        wait(here.at[c, pl.ds(0, 15)], yx_send.at[c])
        return carry

    lax.fori_loop(0, CHUNKS, finish, 0)
    wait(wcol.at[pl.ds(0, 3)], wave_send.at[0])
    wait(whole.at[pl.ds(0, 15)], wave_send.at[1])


def settle(src_ref, dst_ref, held, arrive, leave):
    parts = [pl.ds(i * 1024, 1024) for i in range(8)]
    for i, part in enumerate(parts):
        pltpu.make_async_copy(src_ref.at[part], held.at[part], arrive.at[i]).start()
    for i, part in enumerate(parts):
        pltpu.make_async_copy(src_ref.at[part], held.at[part], arrive.at[i]).wait()
        pltpu.make_async_copy(held.at[part], dst_ref.at[part], leave.at[i]).start()
    for i, part in enumerate(parts):
        pltpu.make_async_copy(held.at[part], dst_ref.at[part], leave.at[i]).wait()


def body(weights, waves, interp):
    node, shift, swap, place = tables()
    any_space = pl.BlockSpec(memory_space=pl.ANY)
    sems = pltpu.SemaphoreType.DMA((CHUNKS,))
    out = pl.pallas_call(
        kernel,
        out_shape=jax.ShapeDtypeStruct((4, 16, CHUNKS, ROWS, 128), jnp.bfloat16),
        in_specs=[any_space] * 7,
        out_specs=any_space,
        scratch_shapes=[
            pltpu.VMEM((CHUNKS, 4, 16, ROWS, 128), jnp.bfloat16),
            pltpu.VMEM((CHUNKS, 16, 4, ROWS, 128), jnp.bfloat16),
            pltpu.VMEM((CHUNKS, 4, 16, ROWS, 128), jnp.bfloat16),
            pltpu.VMEM((4, 2, 2048), jnp.float32),
            pltpu.VMEM((16, 4, 2, 128), jnp.float32),
            pltpu.VMEM((LEVELS, 256, 256), jnp.bfloat16),
            pltpu.VMEM((2, 32, ROWS, 128), jnp.bfloat16),
            pltpu.VMEM((LEVELS, 2, CHUNKS, 32, ROWS, 128), jnp.float32),
            pltpu.VMEM(node.shape, node.dtype),
            pltpu.VMEM(shift.shape, shift.dtype),
            pltpu.VMEM(swap.shape, swap.dtype),
            pltpu.VMEM(place.shape, place.dtype),
            pltpu.VMEM((24, 64, 64), jnp.bfloat16),
            sems, sems, sems, sems, sems, sems, sems, sems,
            pltpu.SemaphoreType.DMA((2,)),
            pltpu.SemaphoreType.DMA((2,)),
            pltpu.SemaphoreType.DMA((5,)),
        ],
        compiler_params=pltpu.CompilerParams(
            collective_id=0, has_side_effects=True, vmem_limit_bytes=56 << 20
        ),
    )(weights.reshape(4, 16, CHUNKS, ROWS, 128), waves, interp.reshape(24, 64, 64), node, shift, swap, place)
    return pl.pallas_call(
        settle,
        out_shape=jax.ShapeDtypeStruct((8192, 128), jnp.bfloat16),
        in_specs=[any_space],
        out_specs=any_space,
        scratch_shapes=[
            pltpu.VMEM((8192, 128), jnp.bfloat16),
            pltpu.SemaphoreType.DMA((8,)),
            pltpu.SemaphoreType.DMA((8,)),
        ],
        compiler_params=pltpu.CompilerParams(vmem_limit_bytes=60 << 20),
    )(out.reshape(8192, 128))


def solution(mesh):
    return jax.shard_map(
        body,
        mesh=mesh,
        in_specs=(P(("bx", "by"), None), P(None, ("bx", "by")), P()),
        out_specs=P(("bx", "by"), None),
        check_vma=False,
    )
```
